32 devices in a mesh: region: 8 (over z, y), member: 4 (over x, core).
Axes of the slice: x: 2, y: 2, z: 4, core: 2. Of those that a mesh axis runs over, the one named last changes fastest.
Arguments:
- control: float32 [64, 4, 128, 512], P('member', None, 'region'), may hold values from -6 to 6
- members: bfloat16 [64, 3, 4, 128, 512], P('member', None, None, 'region'), may hold values from -0.75 to 0.75
- obs_tile: int32 [4096, 1], P('region'), may hold values from 0 to 7; in each aligned block of 512 rows (0 to 511, 512 to 1023, ...) at most 256 rows name the same one
- obs_cell: int32 [4096], P('region'), may hold values from 0 to 98303
- innovation: float32 [4096], P('region'), may hold values from -6 to 6
- obs_weight: float32 [4096], P('region'), may hold values from 1 to 20
Outputs:
- gradient: float32 [64, 4, 128, 512], P('member', None, 'region')
The draws below stay inside these ranges and needn't reach their ends.
Inputs may be any that keep to these rules, and one draw needn't show every extreme that they name: `obs_tile`: among the 512 observations of each device's block, at most 256 name the same tile; in every draw some tile is named by exactly 256 of some block. Tiles receive unequal numbers of observations.
All inputs are finite; a program needn't handle non-finite values.
Results may differ from the reference program's by a relative error of at most 0.0003.
Values may be sent and summed in bfloat16 or wider, within the bound.
A program may use at most 128 MiB of HBM per device.

```python
import math
import jax
import jax.numpy as jnp
import numpy as np
from jax import lax

MEMBERS = 64
HALF = 15
LEV = 4
NT = 3
CX = 16
NY = 512
OBS_DEV = 512
NX = 128
OBS = 4096
N_REGION = 8


def place_ends(drawn, key, low, top_value):
    extent = drawn.shape
    spot = [jax.random.randint(jax.random.fold_in(key, axis), (), 0, extent[axis]) for axis in range(len(extent))]
    drawn = drawn.at[tuple(spot)].set(low)
    longest = extent.index(max(extent))
    spot[longest] = (spot[longest] + 1) % extent[longest]
    return drawn.at[tuple(spot)].set(top_value)


def block_scale(key, dims, split, least, high):
    level = 1.0
    for axis_at, shards_of in split:
        heights = jax.random.uniform(jax.random.fold_in(jax.random.fold_in(key, 6), axis_at), (shards_of,), jnp.float32, least / len(split), high / len(split))
        level = level * jnp.repeat(jnp.exp(heights), dims[axis_at] // shards_of).reshape((-1,) + (1,) * (len(dims) - 1 - axis_at))
    return level


def assign_block(rng, own, number, rows, count, top, most, slope):
    order = jax.random.permutation(rng, count)
    heavy_load, usual = shares(count, rows * top, most, slope, True), shares(count, rows * top, most, slope, False)
    places = jnp.arange(count)

    def named(sizes, rotation):
        used = int((sizes > 0).sum())
        fixed = max(1, used // 4)
        shifted = fixed + (places - fixed + rotation * (used - fixed)) % max(1, count - fixed)
        return jnp.zeros((count,), jnp.int32).at[order[jnp.where(places < fixed, places, shifted)]].set(jnp.asarray(sizes, jnp.int32))

    sizes = jnp.where(number % 4 == 0, named(heavy_load, number // 4), named(usual, number - number // 4 - 1))
    mixed = jax.random.permutation(jax.random.fold_in(own, 3), count)
    giver, receiver = mixed[0:count // 2 * 2:2], mixed[1:count // 2 * 2:2]
    slack = jnp.minimum(sizes[giver] - 1, most - sizes[receiver]) // 2
    slack = jnp.where((giver == order[0]) | (receiver == order[0]) | (sizes[receiver] == 0), 0, jnp.maximum(slack, 0))
    shifted = jax.random.randint(jax.random.fold_in(own, 4), (count // 2,), 0, 1 << 20) % (slack + 1)
    sizes = sizes.at[giver].add(-shifted).at[receiver].add(shifted)
    items = jnp.searchsorted(jnp.cumsum(sizes), jnp.arange(rows * top), side="right").astype(jnp.int32)
    table = items.reshape(top, rows).T
    table = table[jax.random.permutation(jax.random.fold_in(own, 1), rows)]
    rotation = jax.random.randint(jax.random.fold_in(own, 2), (rows, 1), 0, top)
    return jnp.take_along_axis(table, (jnp.arange(top)[None, :] + rotation) % top, axis=1)


def shares(count, total, bound, skew, full):
    portions = [(1 << 20) // math.isqrt(grade ** skew) + 1 for grade in range(1, count + 1)]
    largest = bound if full else min(bound, max(-(-total // count), total * portions[0] // sum(portions)))
    least = 1 if total - largest >= count - 1 else 0
    holding, rest = [largest] + [least] * (count - 1), total - largest - least * (count - 1)
    while rest > 0:
        candidates = [i for i in range(1, count) if holding[i] < largest] or [i for i in range(1, count) if holding[i] < bound]
        pool, budget = sum([portions[i] for i in candidates]), rest
        for i in candidates:
            extra = min(bound - holding[i], max(1, budget * portions[i] // pool), rest)
            holding[i] = holding[i] + extra
            rest = rest - extra
    return np.array(holding)


def normal_values(stream_key, shape, deviation, most, pieces=(), held_as=jnp.bfloat16):
    result = deviation * jax.random.normal(stream_key, shape, jnp.float32)
    if pieces:
        result = result * block_scale(stream_key, shape, pieces, -0.22, 0.18)
    return jnp.clip(result, -most, most).astype(held_as)


def setup_inputs(seed: int = 0) -> dict:
    arg_keys = jax.random.split(jax.random.key(seed), 7)
    control = normal_values(arg_keys[0], (MEMBERS, LEV, NX, NY), 1.0, 6.0, ((0, 4), (2, 8)), jnp.float32)
    members = normal_values(arg_keys[1], (MEMBERS, NT, LEV, NX, NY), 0.125, 0.75, ((0, 4), (3, 8)))
    obs_tile_keys = jax.random.split(jax.random.fold_in(arg_keys[2], 1), OBS // OBS_DEV)
    obs_tile_turns = jax.random.permutation(jax.random.fold_in(arg_keys[2], 3), OBS // OBS_DEV)
    obs_tile = jax.vmap(lambda own, number: assign_block(jax.random.fold_in(arg_keys[2], 2), own, number, OBS_DEV, N_REGION, 1, 4 * OBS_DEV // N_REGION, 2))(obs_tile_keys, obs_tile_turns).reshape((OBS, 1))
    obs_cell = place_ends(jax.random.randint(arg_keys[3], (OBS,), 0, NT * LEV * CX * NY), jax.random.fold_in(arg_keys[3], 1), 0, (NT * LEV * CX * NY) - 1).astype(jnp.int32)
    innovation = normal_values(arg_keys[4], (OBS,), 1.0, 6.0, ((0, 8),), jnp.float32)
    obs_weight = jnp.clip(jnp.exp(math.log(20.0) - 2.9957323 * jax.random.uniform(arg_keys[5], (OBS,), jnp.float32) ** block_scale(arg_keys[5], (OBS,), ((0, 8),), -0.2, 0.2)), 1.0, 20.0)
    return {"control": control, "members": members, "obs_tile": obs_tile, "obs_cell": obs_cell, "innovation": innovation, "obs_weight": obs_weight}


def tap_weight(dist):
    span = jnp.arange(-HALF, HALF + 1).astype(jnp.float32)
    total = jnp.sqrt(jnp.sum(jnp.exp(-span * span / 36.0)))
    return jnp.exp(-dist * dist / 72.0) / total

def band_table(count):
    rows = jnp.arange(count)[:, None]
    cols = jnp.arange(count)[None, :]
    dist = (cols - rows).astype(jnp.float32)
    return jnp.where(jnp.abs(cols - rows) <= HALF, tap_weight(dist), 0.0).astype(jnp.float32)

def reference(control, members, obs_tile, obs_cell, innovation, obs_weight):
    table = band_table(NY)

    def smooth(field):
        across = jnp.zeros_like(field)
        for dist in range(-HALF, HALF + 1):
            across = across + tap_weight(jnp.float32(dist)) * jnp.roll(field, -dist, axis=1)
        return jnp.einsum('liy,yz->liz', across, table, precision=lax.Precision.HIGHEST)

    def accumulate(carry, pair):
        field, pert = pair
        return (carry + pert.astype(jnp.float32) * smooth(field)[None], None)
    start = jnp.zeros((NT, LEV, NX, NY), jnp.float32)
    increment, _ = lax.scan(accumulate, start, (control, members))
    tiles_flat = increment.reshape(NT, LEV, N_REGION, CX, NY).transpose(2, 0, 1, 3, 4).reshape(N_REGION, -1)
    owner = obs_tile[:, 0]
    modelled = tiles_flat[owner, obs_cell]
    weighted = obs_weight * (modelled - innovation)
    adjoint_flat = jnp.zeros_like(tiles_flat).at[owner, obs_cell].add(weighted)
    adjoint = adjoint_flat.reshape(N_REGION, NT, LEV, CX, NY).transpose(1, 2, 0, 3, 4).reshape(NT, LEV, NX, NY)

    def one_member(pair):
        field, pert = pair
        back = lax.optimization_barrier(jnp.sum(pert.astype(jnp.float32) * adjoint, axis=0))
        return field + smooth(back)
    return lax.map(one_member, (control, members))
```

```python
import functools
import math

import jax
import jax.numpy as jnp
from jax import lax
from jax.experimental import pallas as pl
from jax.experimental.pallas import tpu as pltpu
from jax.sharding import PartitionSpec as P

HALF = 15
CHUNK = 256
NORM = math.sqrt(sum(math.exp(-e * e / 36.0) for e in range(-HALF, HALF + 1)))
LIMIT = 40 * 1024 * 1024
NT_DIMS = (((1,), (1,)), ((), ()))


def band_table(count):
    step = jnp.arange(count)[None, :] - jnp.arange(count)[:, None]
    dist = step.astype(jnp.float32)
    return jnp.where(jnp.abs(step) <= HALF, jnp.exp(-dist * dist / 72.0) / NORM, 0.0)


def dot(a, b):
    return jnp.dot(a, b, preferred_element_type=jnp.float32)


def dot_nt(a, b):
    return lax.dot_general(a, b, NT_DIMS, preferred_element_type=jnp.float32)


def halves(value):
    high = value.astype(jnp.bfloat16)
    low = (value - high.astype(jnp.float32)).astype(jnp.bfloat16)
    return high, low


def filter_rows(value, table_high, table_low):
    high, low = halves(value)
    return dot(high, table_high) + (dot(high, table_low) + dot(low, table_high))


def cells_of(cell, shape):
    _, lev, width_x, width_y = shape
    y = lax.rem(cell, width_y)
    column = lax.div(cell, width_y)
    x = lax.rem(column, width_x)
    level = lax.rem(lax.div(column, width_x), lev)
    return y, column, x, level


def latitude_kernel(control_ref, high_ref, low_ref, out_high_ref, out_low_ref):
    filtered = filter_rows(control_ref[...], high_ref[...], low_ref[...])
    out_high_ref[...], out_low_ref[...] = halves(filtered)


def collect_kernel(shape, block, counts_ref, rank_ref, values_ref, members_ref, list_ref, mv_ref):
    _, _, _, width_y = shape
    group = math.prod(shape[:3])
    per_dev = members_ref.shape[0] // group
    base = pl.program_id(0) * CHUNK
    count = counts_ref[1]

    @pl.when(base >= count)
    def _():
        list_ref[...] = jnp.zeros_like(list_ref)
        mv_ref[...] = jnp.zeros_like(mv_ref)

    @pl.when(base < count)
    def _():
        slot = base + lax.broadcasted_iota(jnp.int32, (CHUNK, block), 0)

        def step(index, total):
            span = pl.ds(pl.multiple_of(index * block, block), block)
            pick = (rank_ref[:, span] == slot).astype(jnp.float32).astype(jnp.bfloat16)
            value = values_ref[:, span]
            first = value.astype(jnp.bfloat16).astype(jnp.float32)
            rest = value - first
            second = rest.astype(jnp.bfloat16).astype(jnp.float32)
            third = rest - second
            parts = jnp.concatenate([first, second, third], axis=0).astype(jnp.bfloat16)
            return total + dot_nt(parts, pick)

        start = jnp.zeros((24, CHUNK), jnp.float32)
        total = lax.fori_loop(0, rank_ref.shape[1] // block, step, start)
        found = total[0:8] + total[8:16] + total[16:24]
        list_ref[...] = found
        cell = found[0:1].astype(jnp.int32)
        y, column, _, _ = cells_of(cell, shape)
        live = base + lax.broadcasted_iota(jnp.int32, (1, CHUNK), 1) < count
        column = jnp.where(live, column, -1)
        hot = (lax.broadcasted_iota(jnp.int32, (width_y, CHUNK), 0) == y)
        hot = hot.astype(jnp.float32).astype(jnp.bfloat16)
        wanted = lax.broadcasted_iota(jnp.int32, (group, CHUNK), 0) == column
        rows = []
        for m in range(per_dev):
            here = dot(members_ref[m * group:(m + 1) * group], hot)
            rows.append(jnp.sum(jnp.where(wanted, here, 0.0), axis=0, keepdims=True))
        mv_ref[...] = jnp.concatenate(rows, axis=0).astype(jnp.bfloat16)


def footprint(shape, cell, side):
    _, lev, width_x, width_y = shape
    y, _, x, level = cells_of(cell, shape)
    hot = (lax.broadcasted_iota(jnp.int32, (width_y, CHUNK), 0) == y)
    hot = hot.astype(jnp.float32).astype(jnp.bfloat16)
    row = lax.broadcasted_iota(jnp.int32, (lev * width_x, CHUNK), 0)
    step = x + (side - 1) * width_x - lax.rem(row, width_x)
    dist = step.astype(jnp.float32)
    near = (jnp.abs(step) <= HALF) & (lax.div(row, width_x) == level)
    return hot, jnp.where(near, jnp.exp(-dist * dist / 72.0) * (1.0 / NORM), 0.0)


def sample_kernel(shape, counts_ref, list_ref, mv_ref, high_ref, low_ref, out_ref):
    side, base = pl.program_id(0), pl.program_id(1) * CHUNK
    count = counts_ref[side]
    plane = shape[1] * shape[2]
    per_dev = mv_ref.shape[1]
    group = max(1, 256 // plane)

    @pl.when(base >= count)
    def _():
        out_ref[...] = jnp.zeros_like(out_ref)

    @pl.when(base < count)
    def _():
        hot, across = footprint(shape, list_ref[0, 0:1].astype(jnp.int32), side)
        mv = mv_ref[0].astype(jnp.float32)
        total = jnp.zeros((plane, CHUNK), jnp.float32)
        for m in range(0, per_dev, group):
            rows = slice(m * plane, (m + group) * plane)
            here = dot(high_ref[rows], hot) + dot(low_ref[rows], hot)
            for k in range(group):
                total += here[k * plane:(k + 1) * plane] * mv[m + k:m + k + 1]
        out_ref[0] = jnp.sum(total * across, axis=0, keepdims=True)


def spread_kernel(
    shape, counts_ref, list_ref, mv_ref, weighted_ref, control_ref, high_ref, low_ref, out_ref, acc
):
    side, base = pl.program_id(0), pl.program_id(1) * CHUNK
    plane = shape[1] * shape[2]
    per_dev = mv_ref.shape[1]
    group = max(1, 256 // plane)

    @pl.when((side == 0) & (base == 0))
    def _():
        acc[...] = jnp.zeros_like(acc)

    @pl.when(base < counts_ref[side])
    def _():
        hot, across = footprint(shape, list_ref[0, 0:1].astype(jnp.int32), side)
        scaled = mv_ref[0].astype(jnp.float32) * weighted_ref[0]
        for m in range(0, per_dev, group):
            rows = slice(m * plane, (m + group) * plane)
            terms = [across * scaled[m + k:m + k + 1] for k in range(group)]
            high, low = halves(jnp.concatenate(terms, axis=0))
            acc[rows] += dot_nt(high, hot) + dot_nt(low, hot)

    @pl.when((side == 2) & (base + CHUNK == pl.num_programs(1) * CHUNK))
    def _():
        for r in range(0, acc.shape[0], 256):
            rows = slice(r, r + 256)
            out_ref[rows] = control_ref[rows] + filter_rows(acc[rows], high_ref[...], low_ref[...])


def local(control, members, obs_tile, obs_cell, innovation, obs_weight):
    per_dev, times, lev, width_x, width_y = members.shape
    shape = (times, lev, width_x, width_y)
    rows = per_dev * lev * width_x
    regions = lax.axis_size("region")
    me = lax.axis_index("region")
    obs_dev = obs_cell.shape[0]
    capacity = regions * (4 * obs_dev // regions)
    slots = -(-capacity // CHUNK) * CHUNK
    chunks = slots // CHUNK
    params = pltpu.CompilerParams(vmem_limit_bytes=LIMIT)
    f32, bf16 = jnp.float32, jnp.bfloat16

    packed = jnp.stack(
        [obs_cell.astype(f32), innovation, obs_weight, obs_tile[:, 0].astype(f32)]
    )
    every = lax.all_gather(packed, "region", axis=1, tiled=True)
    total = every.shape[1]

    table = band_table(width_y)
    table_high = lax.reduce_precision(table, 8, 7)
    table_low = (table - table_high).astype(bf16)
    table_high = table_high.astype(bf16)
    flat = control.reshape(rows, width_y)
    whole_table = pl.BlockSpec((width_y, width_y), lambda i: (0, 0))
    part = pl.BlockSpec((256, width_y), lambda i: (i, 0))
    field_high, field_low = pl.pallas_call(
        latitude_kernel,
        grid=(rows // 256,),
        in_specs=[part, whole_table, whole_table],
        out_specs=[part, part],
        out_shape=[jax.ShapeDtypeStruct((rows, width_y), bf16)] * 2,
        compiler_params=params,
        cost_estimate=pl.CostEstimate(
            flops=6 * rows * width_y * width_y, bytes_accessed=8 * rows * width_y, transcendentals=0
        ),
        name="latitude_filter",
    )(flat, table_high, table_low)

    owner = every[3].astype(jnp.int32)
    sides = lax.rem(me + regions + jnp.arange(-1, 2), regions)
    counts = jnp.sum((owner[None] == sides[:, None]).astype(jnp.int32), axis=1)
    mine = (owner == me).astype(f32).reshape(total // 128, 128)
    upper = (jnp.arange(128)[:, None] <= jnp.arange(128)[None, :]).astype(f32)
    inside = jnp.dot(mine, upper)
    line = jnp.arange(total // 128)
    earlier = (line[:, None] > line[None, :]).astype(f32)
    before = jnp.sum(earlier * inside[:, 127][None, :], axis=1)
    rank = jnp.where(mine > 0, (inside + before[:, None]).astype(jnp.int32) - 1, -1)
    rank = rank.reshape(1, total)
    values = jnp.concatenate([every[:3], jnp.zeros((5, total), f32)], axis=0)
    block = next(b for b in (4096, 2048, 1024, 512, 256, 128) if total % b == 0)

    listed, mv = pl.pallas_call(
        functools.partial(collect_kernel, shape, block),
        grid_spec=pltpu.PrefetchScalarGridSpec(
            num_scalar_prefetch=1,
            grid=(chunks,),
            in_specs=[
                pl.BlockSpec((1, total), lambda j, c: (0, 0)),
                pl.BlockSpec((8, total), lambda j, c: (0, 0)),
                pl.BlockSpec((per_dev * times * lev * width_x, width_y), lambda j, c: (0, 0)),
            ],
            out_specs=[
                pl.BlockSpec((8, CHUNK), lambda j, c: (0, j)),
                pl.BlockSpec((per_dev, CHUNK), lambda j, c: (0, j)),
            ],
        ),
        out_shape=[
            jax.ShapeDtypeStruct((8, slots), f32),
            jax.ShapeDtypeStruct((per_dev, slots), bf16),
        ],
        compiler_params=params,
        name="collect_members",
    )(counts, rank, values, members.reshape(-1, width_y))

    def shifted(value, by):
        pairs = [(i, (i + by) % regions) for i in range(regions)]
        return lax.ppermute(value, "region", pairs)

    short = listed[:3]
    lists = jnp.stack([shifted(short, 1), short, shifted(short, -1)])
    mvs = jnp.stack([shifted(mv, 1), mv, shifted(mv, -1)])

    list_spec = pl.BlockSpec((1, 3, CHUNK), lambda q, j, c: (q, 0, j))
    mv_spec = pl.BlockSpec((1, per_dev, CHUNK), lambda q, j, c: (q, 0, j))
    row_spec = pl.BlockSpec((1, 1, CHUNK), lambda q, j, c: (q, 0, j))
    field_spec = pl.BlockSpec((rows, width_y), lambda q, j, c: (0, 0))
    table_spec = pl.BlockSpec((width_y, width_y), lambda q, j, c: (0, 0))
    partial = pl.pallas_call(
        functools.partial(sample_kernel, shape),
        grid_spec=pltpu.PrefetchScalarGridSpec(
            num_scalar_prefetch=1,
            grid=(3, chunks),
            in_specs=[list_spec, mv_spec, field_spec, field_spec],
            out_specs=row_spec,
        ),
        out_shape=jax.ShapeDtypeStruct((3, 1, slots), f32),
        compiler_params=params,
        name="sample_increment",
    )(counts, lists, mvs, field_high, field_low)[:, 0]

    partial = lax.psum(partial, "member")
    up1 = shifted(partial[1:], 1)
    down1 = shifted(partial[:2], -1)
    up2 = shifted(partial[2], 2)
    down2 = shifted(partial[0], -2)
    modelled = partial + jnp.stack([up1[0] + up2, up1[1] + down1[0], down1[1] + down2])
    weighted = lists[:, 2] * (modelled - lists[:, 1])

    result = pl.pallas_call(
        functools.partial(spread_kernel, shape),
        grid_spec=pltpu.PrefetchScalarGridSpec(
            num_scalar_prefetch=1,
            grid=(3, chunks),
            in_specs=[
                list_spec, mv_spec, row_spec, field_spec, table_spec, table_spec,
            ],
            out_specs=field_spec,
            scratch_shapes=[pltpu.VMEM((rows, width_y), f32)],
        ),
        out_shape=jax.ShapeDtypeStruct((rows, width_y), f32),
        compiler_params=params,
        name="spread_adjoint",
    )(counts, lists, mvs, weighted[:, None], flat, table_high, table_low)
    return result.reshape(control.shape)


def solution(mesh):
    placed = (
        P("member", None, "region", None),
        P("member", None, None, "region", None),
        P("region", None),
        P("region"),
        P("region"),
        P("region"),
    )
    return jax.shard_map(
        local,
        mesh=mesh,
        in_specs=placed,
        out_specs=P("member", None, "region", None),
        check_vma=False,
    )
```

```python
import functools
import math

import jax
import jax.numpy as jnp
from jax import lax
from jax.experimental import pallas as pl
from jax.experimental.pallas import tpu as pltpu
from jax.sharding import PartitionSpec as P

HALF = 15
CHUNK = 256
NORM = math.sqrt(sum(math.exp(-e * e / 36.0) for e in range(-HALF, HALF + 1)))
LIMIT = 40 * 1024 * 1024
MESH = pl.DeviceIdType.MESH
NT_DIMS = (((1,), (1,)), ((), ()))


def band_table(count):
    step = jnp.arange(count)[None, :] - jnp.arange(count)[:, None]
    dist = step.astype(jnp.float32)
    return jnp.where(jnp.abs(step) <= HALF, jnp.exp(-dist * dist / 72.0) / NORM, 0.0)


def dot(a, b):
    return jnp.dot(a, b, preferred_element_type=jnp.float32)


def dot_nt(a, b):
    return lax.dot_general(a, b, NT_DIMS, preferred_element_type=jnp.float32)


def halves(value):
    high = value.astype(jnp.bfloat16)
    low = (value - high.astype(jnp.float32)).astype(jnp.bfloat16)
    return high, low


def filter_rows(value, table_high, table_low):
    high, low = halves(value)
    return dot(high, table_high) + (dot(high, table_low) + dot(low, table_high))


def cells_of(cell, shape):
    _, lev, width_x, width_y = shape
    y = lax.rem(cell, width_y)
    column = lax.div(cell, width_y)
    x = lax.rem(column, width_x)
    level = lax.rem(lax.div(column, width_x), lev)
    return y, column, x, level


def meet(peers):
    barrier = pltpu.get_barrier_semaphore()
    for axis, peer in peers:
        pl.semaphore_signal(barrier, inc=1, device_id={axis: peer}, device_id_type=MESH)
    pl.semaphore_wait(barrier, len(peers))


def send(source, target, sems, index, axis, peer):
    copy = pltpu.make_async_remote_copy(
        src_ref=source,
        dst_ref=target,
        send_sem=sems[0].at[index],
        recv_sem=sems[1].at[index],
        device_id={axis: peer},
        device_id_type=MESH,
    )
    copy.start()
    return copy


def others(axis, offsets):
    me, count = lax.axis_index(axis), lax.axis_size(axis)
    return [(axis, lax.rem(me + count + by, count)) for by in offsets]


def gather_kernel(
    regions, packed_ref, control_ref, high_ref, low_ref, every_ref, out_high_ref, out_low_ref,
    landed, send_sems, recv_sems
):
    peers = others("region", range(1, regions))
    meet(peers)
    sems = (send_sems, recv_sems)
    copies = [
        send(packed_ref, landed.at[k], sems, k, *peer) for k, peer in enumerate(peers)
    ]
    for r in range(0, control_ref.shape[0], 256):
        rows = slice(r, r + 256)
        filtered = filter_rows(control_ref[rows], high_ref[...], low_ref[...])
        out_high_ref[rows], out_low_ref[rows] = halves(filtered)
    width = packed_ref.shape[1]
    every_ref[:, :width] = packed_ref[...]
    for k, copy in enumerate(copies):
        copy.wait()
        every_ref[:, (k + 1) * width:(k + 2) * width] = landed[k]


def exchange_kernel(list_ref, mv_ref, lists_ref, mvs_ref, land_list, land_mv, send_sems, recv_sems):
    peers = others("region", (1, -1))
    meet(peers)
    sems = (send_sems, recv_sems)
    copies = []
    for k, peer in enumerate(peers):
        copies.append(send(mv_ref, land_mv.at[k], sems, 2 * k, *peer))
        copies.append(send(list_ref, land_list.at[k], sems, 2 * k + 1, *peer))
    lists_ref[1] = list_ref[...]
    mvs_ref[1] = mv_ref[...]
    for copy in copies:
        copy.wait()
    for k in range(2):
        lists_ref[2 * k] = land_list[k]
        mvs_ref[2 * k] = land_mv[k]


def combine_kernel(
    members, partial_ref, lists_ref, out_ref, landed, total, up, down, far_up, far_down,
    send_sems, recv_sems
):
    same = others("member", range(1, members))
    near = others("region", (1, -1, 2, -2))
    meet(same + near)
    sems = (send_sems, recv_sems)
    copies = [
        send(partial_ref, landed.at[k], sems, k, *peer) for k, peer in enumerate(same)
    ]
    value = partial_ref[...]
    for k, copy in enumerate(copies):
        copy.wait()
        value = value + landed[k]
    total[...] = value
    base = len(same)
    copies = [
        send(total.at[pl.ds(1, 2)], up, sems, base, *near[0]),
        send(total.at[pl.ds(0, 2)], down, sems, base + 1, *near[1]),
        send(total.at[pl.ds(2, 1)], far_up, sems, base + 2, *near[2]),
        send(total.at[pl.ds(0, 1)], far_down, sems, base + 3, *near[3]),
    ]
    for copy in copies:
        copy.wait()
    modelled = (
        total[0] + up[0] + far_up[0], total[1] + up[1] + down[0], total[2] + down[1] + far_down[0]
    )
    for q in range(3):
        out_ref[q] = lists_ref[q, 2:3] * (modelled[q] - lists_ref[q, 1:2])


def chunks_of(count):
    return lax.div(count + CHUNK - 1, CHUNK)


def span_of(index):
    return pl.ds(pl.multiple_of(index * CHUNK, CHUNK), CHUNK)


def collect_kernel(
    shape, counts_ref, starts_ref, rank_ref, values_ref, members_ref, list_ref, mv_ref, found_ref
):
    _, _, _, width_y = shape
    group = math.prod(shape[:3])
    per_dev = members_ref.shape[0] // group
    count = counts_ref[1]
    blocks = starts_ref.shape[0] - 1
    block = rank_ref.shape[1] // blocks
    list_ref[...] = jnp.zeros_like(list_ref)
    mv_ref[...] = jnp.zeros_like(mv_ref)

    @pl.loop(0, chunks_of(count))
    def _(index):
        base = index * CHUNK
        slot = base + lax.broadcasted_iota(jnp.int32, (CHUNK, block), 0)
        found_ref[...] = jnp.zeros_like(found_ref)

        @pl.loop(0, blocks)
        def _(source):
            @pl.when((starts_ref[source] < base + CHUNK) & (starts_ref[source + 1] > base))
            def _():
                span = pl.ds(pl.multiple_of(source * block, block), block)
                pick = (rank_ref[:, span] == slot).astype(jnp.float32).astype(jnp.bfloat16)
                value = values_ref[:, span]
                first = value.astype(jnp.bfloat16).astype(jnp.float32)
                rest = value - first
                second = rest.astype(jnp.bfloat16).astype(jnp.float32)
                third = rest - second
                parts = jnp.concatenate([first, second, third], axis=0).astype(jnp.bfloat16)
                found_ref[...] += dot_nt(parts, pick)

        found = found_ref[0:8] + found_ref[8:16] + found_ref[16:24]
        list_ref[:, span_of(index)] = found
        cell = found[0:1].astype(jnp.int32)
        y, column, _, _ = cells_of(cell, shape)
        live = base + lax.broadcasted_iota(jnp.int32, (1, CHUNK), 1) < count
        column = jnp.where(live, column, -1)
        hot = (lax.broadcasted_iota(jnp.int32, (width_y, CHUNK), 0) == y)
        hot = hot.astype(jnp.float32).astype(jnp.bfloat16)
        wanted = lax.broadcasted_iota(jnp.int32, (group, CHUNK), 0) == column
        rows = []
        for m in range(0, per_dev, 4):
            here = dot(members_ref[m * group:(m + 4) * group], hot)
            for k in range(4):
                one = jnp.where(wanted, here[k * group:(k + 1) * group], 0.0)
                rows.append(jnp.sum(one, axis=0, keepdims=True))
        mv_ref[:, span_of(index)] = jnp.concatenate(rows, axis=0).astype(jnp.bfloat16)


def footprint(shape, cell, side):
    _, lev, width_x, width_y = shape
    y, _, x, level = cells_of(cell, shape)
    hot = (lax.broadcasted_iota(jnp.int32, (width_y, CHUNK), 0) == y)
    hot = hot.astype(jnp.float32).astype(jnp.bfloat16)
    row = lax.broadcasted_iota(jnp.int32, (lev * width_x, CHUNK), 0)
    step = x + (side - 1) * width_x - lax.rem(row, width_x)
    dist = step.astype(jnp.float32)
    near = (jnp.abs(step) <= HALF) & (lax.div(row, width_x) == level)
    return hot, jnp.where(near, jnp.exp(-dist * dist / 72.0) * (1.0 / NORM), 0.0)


def sample_kernel(shape, counts_ref, list_ref, mv_ref, high_ref, low_ref, out_ref):
    plane = shape[1] * shape[2]
    per_dev = mv_ref.shape[1]
    group = max(1, 512 // plane)
    out_ref[...] = jnp.zeros_like(out_ref)
    for side in range(3):

        @pl.loop(0, chunks_of(counts_ref[side]))
        def _(index):
            span = span_of(index)
            hot, across = footprint(shape, list_ref[side, 0:1, span].astype(jnp.int32), side)
            mv = mv_ref[side, :, span].astype(jnp.float32)
            total = jnp.zeros((plane, CHUNK), jnp.float32)
            for m in range(0, per_dev, group):
                rows = slice(m * plane, (m + group) * plane)
                here = dot(high_ref[rows], hot) + dot(low_ref[rows], hot)
                for k in range(group):
                    total += here[k * plane:(k + 1) * plane] * mv[m + k:m + k + 1]
            out_ref[side, :, span] = jnp.sum(total * across, axis=0, keepdims=True)


def spread_kernel(
    shape, counts_ref, list_ref, mv_ref, weighted_ref, control_ref, high_ref, low_ref, out_ref, acc
):
    plane = shape[1] * shape[2]
    per_dev = mv_ref.shape[1]
    group = max(1, 512 // plane)
    acc[...] = jnp.zeros_like(acc)
    for side in range(3):

        @pl.loop(0, chunks_of(counts_ref[side]))
        def _(index):
            span = span_of(index)
            hot, across = footprint(shape, list_ref[side, 0:1, span].astype(jnp.int32), side)
            scaled = mv_ref[side, :, span].astype(jnp.float32) * weighted_ref[side, :, span]
            for m in range(0, per_dev, group):
                rows = slice(m * plane, (m + group) * plane)
                terms = [across * scaled[m + k:m + k + 1] for k in range(group)]
                high, low = halves(jnp.concatenate(terms, axis=0))
                acc[rows] += dot_nt(high, hot) + dot_nt(low, hot)

    for r in range(0, acc.shape[0], 256):
        rows = slice(r, r + 256)
        out_ref[rows] = control_ref[rows] + filter_rows(acc[rows], high_ref[...], low_ref[...])


def local(control, members, obs_tile, obs_cell, innovation, obs_weight):
    per_dev, times, lev, width_x, width_y = members.shape
    shape = (times, lev, width_x, width_y)
    rows = per_dev * lev * width_x
    regions = lax.axis_size("region")
    shares = lax.axis_size("member")
    me = lax.axis_index("region")
    obs_dev = obs_cell.shape[0]
    capacity = regions * (4 * obs_dev // regions)
    slots = -(-capacity // CHUNK) * CHUNK
    total = regions * obs_dev
    f32, bf16, i32 = jnp.float32, jnp.bfloat16, jnp.int32
    like = jax.ShapeDtypeStruct
    vmem = pl.BlockSpec(memory_space=pltpu.VMEM)
    smem = pl.BlockSpec(memory_space=pltpu.SMEM)
    plain = pltpu.CompilerParams(vmem_limit_bytes=LIMIT)
    sems = pltpu.SemaphoreType.DMA

    def remote(number):
        return pltpu.CompilerParams(
            vmem_limit_bytes=LIMIT, collective_id=number, has_side_effects=True
        )

    packed = jnp.concatenate(
        [
            jnp.stack([obs_cell.astype(f32), innovation, obs_weight, obs_tile[:, 0].astype(f32)]),
            jnp.zeros((4, obs_dev), f32),
        ]
    )
    table = band_table(width_y)
    table_high = lax.reduce_precision(table, 8, 7)
    table_low = (table - table_high).astype(bf16)
    table_high = table_high.astype(bf16)
    flat = control.reshape(rows, width_y)
    every, field_high, field_low = pl.pallas_call(
        functools.partial(gather_kernel, regions),
        in_specs=[vmem] * 4,
        out_specs=[vmem] * 3,
        out_shape=[like((8, total), f32), like((rows, width_y), bf16), like((rows, width_y), bf16)],
        scratch_shapes=[
            pltpu.VMEM((regions - 1, 8, obs_dev), f32), sems((regions - 1,)), sems((regions - 1,)),
        ],
        compiler_params=remote(0),
        name="gather_observations",
    )(packed, flat, table_high, table_low)

    owner = every[3].astype(i32)
    sides = lax.rem(me + regions + jnp.arange(-1, 2), regions)
    counts = jnp.sum((owner[None] == sides[:, None]).astype(i32), axis=1)
    mine = (owner == me).astype(f32).reshape(total // 128, 128)
    upper = (jnp.arange(128)[:, None] <= jnp.arange(128)[None, :]).astype(f32)
    inside = jnp.dot(mine, upper)
    line = jnp.arange(total // 128)
    earlier = (line[:, None] > line[None, :]).astype(f32)
    before = jnp.sum(earlier * jnp.sum(mine, axis=1)[None, :], axis=1).astype(i32)
    rank = jnp.where(mine > 0, inside.astype(i32) + before[:, None] - 1, -1).reshape(1, total)
    starts = jnp.concatenate([before[:: obs_dev // 128], counts[1:2]])

    listed, mv = pl.pallas_call(
        functools.partial(collect_kernel, shape),
        in_specs=[smem] * 2 + [vmem] * 3,
        out_specs=[vmem] * 2,
        out_shape=[like((8, slots), f32), like((per_dev, slots), bf16)],
        scratch_shapes=[pltpu.VMEM((24, CHUNK), f32)],
        compiler_params=plain,
        name="collect_members",
    )(counts, starts, rank, every, members.reshape(-1, width_y))

    lists, mvs = pl.pallas_call(
        exchange_kernel,
        in_specs=[vmem] * 2,
        out_specs=[vmem] * 2,
        out_shape=[like((3, 8, slots), f32), like((3, per_dev, slots), bf16)],
        scratch_shapes=[
            pltpu.VMEM((2, 8, slots), f32), pltpu.VMEM((2, per_dev, slots), bf16),
            sems((4,)), sems((4,)),
        ],
        compiler_params=remote(1),
        name="exchange_members",
    )(listed, mv)

    partial = pl.pallas_call(
        functools.partial(sample_kernel, shape),
        in_specs=[smem] + [vmem] * 4,
        out_specs=vmem,
        out_shape=like((3, 1, slots), f32),
        compiler_params=plain,
        name="sample_increment",
    )(counts, lists, mvs, field_high, field_low)

    weighted = pl.pallas_call(
        functools.partial(combine_kernel, shares),
        in_specs=[vmem] * 2,
        out_specs=vmem,
        out_shape=like((3, 1, slots), f32),
        scratch_shapes=[
            pltpu.VMEM((shares - 1, 3, 1, slots), f32), pltpu.VMEM((3, 1, slots), f32),
            pltpu.VMEM((2, 1, slots), f32), pltpu.VMEM((2, 1, slots), f32),
            pltpu.VMEM((1, 1, slots), f32), pltpu.VMEM((1, 1, slots), f32),
            sems((shares + 3,)), sems((shares + 3,)),
        ],
        compiler_params=remote(2),
        name="combine_samples",
    )(partial, lists)

    result = pl.pallas_call(
        functools.partial(spread_kernel, shape),
        in_specs=[smem] + [vmem] * 6,
        out_specs=vmem,
        out_shape=like((rows, width_y), f32),
        scratch_shapes=[pltpu.VMEM((rows, width_y), f32)],
        compiler_params=plain,
        name="spread_adjoint",
    )(counts, lists, mvs, weighted, flat, table_high, table_low)
    return result.reshape(control.shape)


def solution(mesh):
    placed = (
        P("member", None, "region", None),
        P("member", None, None, "region", None),
        P("region", None),
        P("region"),
        P("region"),
        P("region"),
    )
    return jax.shard_map(
        local,
        mesh=mesh,
        in_specs=placed,
        out_specs=P("member", None, "region", None),
        check_vma=False,
    )
```

```python
import functools
import math

import jax
import jax.numpy as jnp
from jax import lax
from jax.experimental import pallas as pl
from jax.experimental.pallas import tpu as pltpu
from jax.sharding import PartitionSpec as P

HALF = 15
CHUNK = 256
NORM = math.sqrt(sum(math.exp(-e * e / 36.0) for e in range(-HALF, HALF + 1)))
LIMIT = 20 * 1024 * 1024
MESH = pl.DeviceIdType.MESH
NT_DIMS = (((1,), (1,)), ((), ()))


def band_table(count):
    shape = (count, count)
    step = lax.broadcasted_iota(jnp.int32, shape, 1) - lax.broadcasted_iota(jnp.int32, shape, 0)
    dist = step.astype(jnp.float32)
    return jnp.where(jnp.abs(step) <= HALF, jnp.exp(-dist * dist / 72.0) * (1.0 / NORM), 0.0)


def dot(a, b):
    return jnp.dot(a, b, preferred_element_type=jnp.float32)


def dot_nt(a, b):
    return lax.dot_general(a, b, NT_DIMS, preferred_element_type=jnp.float32)


def halves(value):
    high = value.astype(jnp.bfloat16)
    low = (value - high.astype(jnp.float32)).astype(jnp.bfloat16)
    return high, low


def filter_rows(value, table_high, table_low):
    high, low = halves(value)
    return dot(high, table_high) + (dot(high, table_low) + dot(low, table_high))


def cells_of(cell, shape):
    _, lev, width_x, width_y = shape
    y = lax.rem(cell, width_y)
    column = lax.div(cell, width_y)
    x = lax.rem(column, width_x)
    level = lax.rem(lax.div(column, width_x), lev)
    return y, column, x, level


def meet(peers):
    barrier = pltpu.get_barrier_semaphore()
    for axis, peer in peers:
        pl.semaphore_signal(barrier, inc=1, device_id={axis: peer}, device_id_type=MESH)
    pl.semaphore_wait(barrier, len(peers))


def send(source, target, sems, index, axis, peer):
    copy = pltpu.make_async_remote_copy(
        src_ref=source,
        dst_ref=target,
        send_sem=sems[0].at[index],
        recv_sem=sems[1].at[index],
        device_id={axis: peer},
        device_id_type=MESH,
    )
    copy.start()
    return copy


def others(axis, offsets):
    me, count = lax.axis_index(axis), lax.axis_size(axis)
    return [(axis, lax.rem(me + count + by, count)) for by in offsets]


def gather_kernel(
    regions, packed_ref, control_ref, every_ref, rank_ref, starts_ref, counts_ref,
    out_high_ref, out_low_ref, high_ref, low_ref, landed, send_sems, recv_sems
):
    peers = others("region", range(1, regions))
    meet(peers)
    sems = (send_sems, recv_sems)
    copies = [
        send(packed_ref, landed.at[k], sems, k, *peer) for k, peer in enumerate(peers)
    ]
    high_ref[...], low_ref[...] = halves(band_table(control_ref.shape[1]))
    for r in range(0, control_ref.shape[0], 256):
        rows = slice(r, r + 256)
        filtered = filter_rows(control_ref[rows], high_ref[...], low_ref[...])
        out_high_ref[rows], out_low_ref[rows] = halves(filtered)
    width = packed_ref.shape[1]
    every_ref[0] = packed_ref[...]
    for k, copy in enumerate(copies):
        copy.wait()
        every_ref[k + 1] = landed[k]

    me = lax.axis_index("region")
    owner = [every_ref[k, 3:4] for k in range(regions)]
    mine = [(o.astype(jnp.int32) == me).astype(jnp.float32) for o in owner]
    mask = jnp.concatenate(mine, axis=0)
    order = lax.broadcasted_iota(jnp.int32, (width, width), 0)
    upper = order <= lax.broadcasted_iota(jnp.int32, (width, width), 1)
    inside = dot(mask.astype(jnp.bfloat16), upper.astype(jnp.float32).astype(jnp.bfloat16))
    lane = lax.broadcasted_iota(jnp.int32, starts_ref.shape, 1)
    starts = jnp.zeros(starts_ref.shape, jnp.float32)
    before = jnp.zeros((1, 1), jnp.float32)
    for k in range(regions):
        starts = jnp.where(lane == k, before, starts)
        rank = jnp.where(mine[k] > 0.5, inside[k:k + 1] + before - 1.0, -1.0)
        rank_ref[k] = rank.astype(jnp.int32)
        before = before + jnp.sum(mine[k], axis=1, keepdims=True)
    starts_ref[...] = jnp.where(lane == regions, before, starts).astype(jnp.int32)
    lane = lax.broadcasted_iota(jnp.int32, counts_ref.shape, 1)
    counts = jnp.zeros(counts_ref.shape, jnp.float32)
    tiles = jnp.concatenate(owner, axis=0).astype(jnp.int32)
    for side in range(3):
        tile = lax.rem(me + regions + side - 1, regions)
        named = jnp.sum((tiles == tile).astype(jnp.float32), axis=0, keepdims=True)
        counts = jnp.where(lane == side, jnp.sum(named, axis=1, keepdims=True), counts)
    counts_ref[...] = counts.astype(jnp.int32)


def exchange_kernel(list_ref, mv_ref, lists_ref, mvs_ref, land_list, land_mv, send_sems, recv_sems):
    peers = others("region", (1, -1))
    meet(peers)
    sems = (send_sems, recv_sems)
    copies = []
    for k, peer in enumerate(peers):
        copies.append(send(mv_ref, land_mv.at[k], sems, 2 * k, *peer))
        copies.append(send(list_ref, land_list.at[k], sems, 2 * k + 1, *peer))
    lists_ref[1] = list_ref[...]
    mvs_ref[1] = mv_ref[...]
    for copy in copies:
        copy.wait()
    for k in range(2):
        lists_ref[2 * k] = land_list[k]
        mvs_ref[2 * k] = land_mv[k]


def combine_kernel(
    members, partial_ref, lists_ref, out_ref, landed, total, up, down, far_up, far_down,
    send_sems, recv_sems
):
    same = others("member", range(1, members))
    near = others("region", (1, -1, 2, -2))
    meet(same + near)
    sems = (send_sems, recv_sems)
    copies = [
        send(partial_ref, landed.at[k], sems, k, *peer) for k, peer in enumerate(same)
    ]
    value = partial_ref[...]
    for k, copy in enumerate(copies):
        copy.wait()
        value = value + landed[k]
    total[...] = value
    base = len(same)
    copies = [
        send(total.at[pl.ds(1, 2)], up, sems, base, *near[0]),
        send(total.at[pl.ds(0, 2)], down, sems, base + 1, *near[1]),
        send(total.at[pl.ds(2, 1)], far_up, sems, base + 2, *near[2]),
        send(total.at[pl.ds(0, 1)], far_down, sems, base + 3, *near[3]),
    ]
    for copy in copies:
        copy.wait()
    modelled = (
        total[0] + up[0] + far_up[0], total[1] + up[1] + down[0], total[2] + down[1] + far_down[0]
    )
    for q in range(3):
        out_ref[q] = lists_ref[q, 2] * (modelled[q] - lists_ref[q, 1])


def chunks_of(count):
    return lax.div(count + CHUNK - 1, CHUNK)


def span_of(index):
    return pl.ds(pl.multiple_of(index * CHUNK, CHUNK), CHUNK)


def collect_kernel(
    shape, counts_ref, starts_ref, rank_ref, values_ref, members_ref, list_ref, mv_ref, found_ref
):
    _, _, _, width_y = shape
    group = math.prod(shape[:3])
    per_dev = members_ref.shape[0] // group
    count = counts_ref[0, 1]
    blocks, _, block = rank_ref.shape
    list_ref[...] = jnp.zeros_like(list_ref)
    mv_ref[...] = jnp.zeros_like(mv_ref)

    @pl.loop(0, chunks_of(count))
    def _(index):
        base = index * CHUNK
        slot = base + lax.broadcasted_iota(jnp.int32, (CHUNK, block), 0)
        found_ref[...] = jnp.zeros_like(found_ref)

        @pl.loop(0, blocks)
        def _(source):
            @pl.when((starts_ref[0, source] < base + CHUNK) & (starts_ref[0, source + 1] > base))
            def _():
                pick = (rank_ref[source] == slot).astype(jnp.float32).astype(jnp.bfloat16)
                value = values_ref[source]
                first = value.astype(jnp.bfloat16).astype(jnp.float32)
                rest = value - first
                second = rest.astype(jnp.bfloat16).astype(jnp.float32)
                third = rest - second
                parts = jnp.concatenate([first, second, third], axis=0).astype(jnp.bfloat16)
                found_ref[...] += dot_nt(parts, pick)

        found = found_ref[0:8] + found_ref[8:16] + found_ref[16:24]
        for row in range(3):
            list_ref[row, :, span_of(index)] = found[row:row + 1]
        cell = found[0:1].astype(jnp.int32)
        y, column, _, _ = cells_of(cell, shape)
        live = base + lax.broadcasted_iota(jnp.int32, (1, CHUNK), 1) < count
        column = jnp.where(live, column, -1)
        hot = (lax.broadcasted_iota(jnp.int32, (width_y, CHUNK), 0) == y)
        hot = hot.astype(jnp.float32).astype(jnp.bfloat16)
        wanted = lax.broadcasted_iota(jnp.int32, (group, CHUNK), 0) == column
        rows = []
        for m in range(0, per_dev, 4):
            here = dot(members_ref[m * group:(m + 4) * group], hot)
            for k in range(4):
                one = jnp.where(wanted, here[k * group:(k + 1) * group], 0.0)
                rows.append(jnp.sum(one, axis=0, keepdims=True))
        mv_ref[:, span_of(index)] = jnp.concatenate(rows, axis=0).astype(jnp.bfloat16)


def footprint(shape, cell, side):
    _, lev, width_x, width_y = shape
    y, _, x, level = cells_of(cell, shape)
    hot = (lax.broadcasted_iota(jnp.int32, (width_y, CHUNK), 0) == y)
    hot = hot.astype(jnp.float32).astype(jnp.bfloat16)
    row = lax.broadcasted_iota(jnp.int32, (lev * width_x, CHUNK), 0)
    step = x + (side - 1) * width_x - lax.rem(row, width_x)
    dist = step.astype(jnp.float32)
    near = (jnp.abs(step) <= HALF) & (lax.div(row, width_x) == level)
    return hot, jnp.where(near, jnp.exp(-dist * dist / 72.0) * (1.0 / NORM), 0.0)


def sample_kernel(shape, counts_ref, list_ref, mv_ref, high_ref, low_ref, out_ref):
    plane = shape[1] * shape[2]
    per_dev = mv_ref.shape[1]
    group = max(1, 512 // plane)
    out_ref[...] = jnp.zeros_like(out_ref)
    for side in range(3):

        @pl.loop(0, chunks_of(counts_ref[0, side]))
        def _(index):
            span = span_of(index)
            hot, across = footprint(shape, list_ref[side, 0, :, span].astype(jnp.int32), side)
            mv = mv_ref[side, :, span].astype(jnp.float32)
            total = jnp.zeros((plane, CHUNK), jnp.float32)
            for m in range(0, per_dev, group):
                rows = slice(m * plane, (m + group) * plane)
                here = dot(high_ref[rows], hot) + dot(low_ref[rows], hot)
                for k in range(group):
                    total += here[k * plane:(k + 1) * plane] * mv[m + k:m + k + 1]
            out_ref[side, :, span] = jnp.sum(total * across, axis=0, keepdims=True)


def spread_kernel(
    shape, counts_ref, list_ref, mv_ref, weighted_ref, control_ref, high_ref, low_ref, out_ref, acc
):
    plane = shape[1] * shape[2]
    per_dev = mv_ref.shape[1]
    group = max(1, 512 // plane)
    acc[...] = jnp.zeros_like(acc)
    for side in range(3):

        @pl.loop(0, chunks_of(counts_ref[0, side]))
        def _(index):
            span = span_of(index)
            hot, across = footprint(shape, list_ref[side, 0, :, span].astype(jnp.int32), side)
            scaled = mv_ref[side, :, span].astype(jnp.float32) * weighted_ref[side, :, span]
            for m in range(0, per_dev, group):
                rows = slice(m * plane, (m + group) * plane)
                terms = [across * scaled[m + k:m + k + 1] for k in range(group)]
                high, low = halves(jnp.concatenate(terms, axis=0))
                acc[rows] += dot_nt(high, hot) + dot_nt(low, hot)

    for r in range(0, acc.shape[0], 256):
        rows = slice(r, r + 256)
        out_ref[rows] = control_ref[rows] + filter_rows(acc[rows], high_ref[...], low_ref[...])


def local(control, members, obs_tile, obs_cell, innovation, obs_weight):
    per_dev, times, lev, width_x, width_y = members.shape
    shape = (times, lev, width_x, width_y)
    rows = per_dev * lev * width_x
    regions = lax.axis_size("region")
    shares = lax.axis_size("member")
    obs_dev = obs_cell.shape[0]
    capacity = regions * (4 * obs_dev // regions)
    slots = -(-capacity // CHUNK) * CHUNK
    f32, bf16, i32 = jnp.float32, jnp.bfloat16, jnp.int32
    like = jax.ShapeDtypeStruct
    vmem = pl.BlockSpec(memory_space=pltpu.VMEM)
    smem = pl.BlockSpec(memory_space=pltpu.SMEM)
    plain = pltpu.CompilerParams(vmem_limit_bytes=LIMIT)
    sems = pltpu.SemaphoreType.DMA

    def remote(number):
        return pltpu.CompilerParams(
            vmem_limit_bytes=LIMIT, collective_id=number, has_side_effects=True
        )

    packed = jnp.concatenate(
        [
            jnp.stack([obs_cell.astype(f32), innovation, obs_weight, obs_tile[:, 0].astype(f32)]),
            jnp.zeros((4, obs_dev), f32),
        ]
    )
    flat = control.reshape(rows, width_y)
    span = -(-(regions + 1) // 128) * 128
    field, table = like((rows, width_y), bf16), like((width_y, width_y), bf16)
    every, rank, starts, counts, field_high, field_low, table_high, table_low = pl.pallas_call(
        functools.partial(gather_kernel, regions),
        in_specs=[vmem] * 2,
        out_specs=[vmem] * 8,
        out_shape=[
            like((regions, 8, obs_dev), f32), like((regions, 1, obs_dev), i32),
            like((1, span), i32), like((1, 128), i32), field, field, table, table,
        ],
        scratch_shapes=[
            pltpu.VMEM((regions - 1, 8, obs_dev), f32), sems((regions - 1,)), sems((regions - 1,)),
        ],
        compiler_params=remote(0),
        name="gather_observations",
    )(packed, flat)

    listed, mv = pl.pallas_call(
        functools.partial(collect_kernel, shape),
        in_specs=[smem] * 2 + [vmem] * 3,
        out_specs=[vmem] * 2,
        out_shape=[like((3, 1, slots), f32), like((per_dev, slots), bf16)],
        scratch_shapes=[pltpu.VMEM((24, CHUNK), f32)],
        compiler_params=plain,
        name="collect_members",
    )(counts, starts, rank, every, members.reshape(-1, width_y))

    lists, mvs = pl.pallas_call(
        exchange_kernel,
        in_specs=[vmem] * 2,
        out_specs=[vmem] * 2,
        out_shape=[like((3, 3, 1, slots), f32), like((3, per_dev, slots), bf16)],
        scratch_shapes=[
            pltpu.VMEM((2, 3, 1, slots), f32), pltpu.VMEM((2, per_dev, slots), bf16),
            sems((4,)), sems((4,)),
        ],
        compiler_params=remote(1),
        name="exchange_members",
    )(listed, mv)

    partial = pl.pallas_call(
        functools.partial(sample_kernel, shape),
        in_specs=[smem] + [vmem] * 4,
        out_specs=vmem,
        out_shape=like((3, 1, slots), f32),
        compiler_params=plain,
        name="sample_increment",
    )(counts, lists, mvs, field_high, field_low)

    weighted = pl.pallas_call(
        functools.partial(combine_kernel, shares),
        in_specs=[vmem] * 2,
        out_specs=vmem,
        out_shape=like((3, 1, slots), f32),
        scratch_shapes=[
            pltpu.VMEM((shares - 1, 3, 1, slots), f32), pltpu.VMEM((3, 1, slots), f32),
            pltpu.VMEM((2, 1, slots), f32), pltpu.VMEM((2, 1, slots), f32),
            pltpu.VMEM((1, 1, slots), f32), pltpu.VMEM((1, 1, slots), f32),
            sems((shares + 3,)), sems((shares + 3,)),
        ],
        compiler_params=remote(2),
        name="combine_samples",
    )(partial, lists)

    result = pl.pallas_call(
        functools.partial(spread_kernel, shape),
        in_specs=[smem] + [vmem] * 6,
        out_specs=vmem,
        out_shape=like((rows, width_y), f32),
        scratch_shapes=[pltpu.VMEM((rows, width_y), f32)],
        compiler_params=plain,
        name="spread_adjoint",
    )(counts, lists, mvs, weighted, flat, table_high, table_low)
    return result.reshape(control.shape)


def solution(mesh):
    placed = (
        P("member", None, "region", None),
        P("member", None, None, "region", None),
        P("region", None),
        P("region"),
        P("region"),
        P("region"),
    )
    return jax.shard_map(
        local,
        mesh=mesh,
        in_specs=placed,
        out_specs=P("member", None, "region", None),
        check_vma=False,
    )
```

```python
import functools
import math

import jax
import jax.numpy as jnp
from jax import lax
from jax.experimental import pallas as pl
from jax.experimental.pallas import tpu as pltpu
from jax.sharding import PartitionSpec as P

HALF = 15
CHUNK = 256
NORM = math.sqrt(sum(math.exp(-e * e / 36.0) for e in range(-HALF, HALF + 1)))
LIMIT = 20 * 1024 * 1024
MESH = pl.DeviceIdType.MESH
NT_DIMS = (((1,), (1,)), ((), ()))


def band_table(count):
    shape = (count, count)
    step = lax.broadcasted_iota(jnp.int32, shape, 1) - lax.broadcasted_iota(jnp.int32, shape, 0)
    dist = step.astype(jnp.float32)
    return jnp.where(jnp.abs(step) <= HALF, jnp.exp(-dist * dist / 72.0) * (1.0 / NORM), 0.0)


def dot(a, b):
    return jnp.dot(a, b, preferred_element_type=jnp.float32)


def dot_nt(a, b):
    return lax.dot_general(a, b, NT_DIMS, preferred_element_type=jnp.float32)


def halves(value):
    high = value.astype(jnp.bfloat16)
    low = (value - high.astype(jnp.float32)).astype(jnp.bfloat16)
    return high, low


def filter_rows(value, table_high, table_low):
    high, low = halves(value)
    return dot(high, table_high) + (dot(high, table_low) + dot(low, table_high))


def cells_of(cell, shape):
    _, lev, width_x, width_y = shape
    y = lax.rem(cell, width_y)
    column = lax.div(cell, width_y)
    x = lax.rem(column, width_x)
    level = lax.rem(lax.div(column, width_x), lev)
    return y, column, x, level


def meet(peers):
    barrier = pltpu.get_barrier_semaphore()
    for axis, peer in peers:
        pl.semaphore_signal(barrier, inc=1, device_id={axis: peer}, device_id_type=MESH)
    pl.semaphore_wait(barrier, len(peers))


def send(source, target, sems, index, axis, peer):
    copy = pltpu.make_async_remote_copy(
        src_ref=source,
        dst_ref=target,
        send_sem=sems[0].at[index],
        recv_sem=sems[1].at[index],
        device_id={axis: peer},
        device_id_type=MESH,
    )
    copy.start()
    return copy


def others(axis, offsets):
    me, count = lax.axis_index(axis), lax.axis_size(axis)
    return [(axis, lax.rem(me + count + by, count)) for by in offsets]


def gather_kernel(
    regions, cell_ref, innovation_ref, weight_ref, tile_ref, control_hbm, every_ref, rank_ref, starts_ref, counts_ref,
    out_high_ref, out_low_ref, high_ref, low_ref, packed_ref, control_ref, landed,
    send_sems, recv_sems, fetch_sem
):
    fetch = pltpu.make_async_copy(control_hbm, control_ref, fetch_sem)
    fetch.start()
    packed_ref[...] = jnp.zeros_like(packed_ref)
    packed_ref[0:1] = cell_ref[...].astype(jnp.float32)
    packed_ref[1:2] = innovation_ref[...]
    packed_ref[2:3] = weight_ref[...]
    packed_ref[3:4] = tile_ref[...].astype(jnp.float32)
    peers = others("region", range(1, regions))
    meet(peers)
    sems = (send_sems, recv_sems)
    copies = [
        send(packed_ref, landed.at[k], sems, k, *peer) for k, peer in enumerate(peers)
    ]
    high_ref[...], low_ref[...] = halves(band_table(control_ref.shape[1]))
    fetch.wait()
    for r in range(0, control_ref.shape[0], 256):
        rows = slice(r, r + 256)
        filtered = filter_rows(control_ref[rows], high_ref[...], low_ref[...])
        out_high_ref[rows], out_low_ref[rows] = halves(filtered)
    width = packed_ref.shape[1]
    every_ref[0] = packed_ref[...]
    for k, copy in enumerate(copies):
        copy.wait()
        every_ref[k + 1] = landed[k]

    me = lax.axis_index("region")
    owner = [every_ref[k, 3:4] for k in range(regions)]
    mine = [(o.astype(jnp.int32) == me).astype(jnp.float32) for o in owner]
    mask = jnp.concatenate(mine, axis=0)
    order = lax.broadcasted_iota(jnp.int32, (width, width), 0)
    upper = order <= lax.broadcasted_iota(jnp.int32, (width, width), 1)
    inside = dot(mask.astype(jnp.bfloat16), upper.astype(jnp.float32).astype(jnp.bfloat16))
    lane = lax.broadcasted_iota(jnp.int32, starts_ref.shape, 1)
    starts = jnp.zeros(starts_ref.shape, jnp.float32)
    before = jnp.zeros((1, 1), jnp.float32)
    for k in range(regions):
        starts = jnp.where(lane == k, before, starts)
        rank = jnp.where(mine[k] > 0.5, inside[k:k + 1] + before - 1.0, -1.0)
        rank_ref[k] = rank.astype(jnp.int32)
        before = before + jnp.sum(mine[k], axis=1, keepdims=True)
    starts_ref[...] = jnp.where(lane == regions, before, starts).astype(jnp.int32)
    lane = lax.broadcasted_iota(jnp.int32, counts_ref.shape, 1)
    counts = jnp.zeros(counts_ref.shape, jnp.float32)
    tiles = jnp.concatenate(owner, axis=0).astype(jnp.int32)
    for side in range(3):
        tile = lax.rem(me + regions + side - 1, regions)
        named = jnp.sum((tiles == tile).astype(jnp.float32), axis=0, keepdims=True)
        counts = jnp.where(lane == side, jnp.sum(named, axis=1, keepdims=True), counts)
    counts_ref[...] = counts.astype(jnp.int32)


def exchange_kernel(list_ref, mv_ref, lists_ref, mvs_ref, land_list, land_mv, send_sems, recv_sems):
    peers = others("region", (1, -1))
    meet(peers)
    sems = (send_sems, recv_sems)
    copies = []
    for k, peer in enumerate(peers):
        copies.append(send(mv_ref, land_mv.at[k], sems, 2 * k, *peer))
        copies.append(send(list_ref, land_list.at[k], sems, 2 * k + 1, *peer))
    lists_ref[1] = list_ref[...]
    mvs_ref[1] = mv_ref[...]
    for copy in copies:
        copy.wait()
    for k in range(2):
        lists_ref[2 * k] = land_list[k]
        mvs_ref[2 * k] = land_mv[k]


def combine_kernel(
    members, partial_ref, lists_ref, out_ref, landed, total, up, down, far_up, far_down,
    send_sems, recv_sems
):
    same = others("member", range(1, members))
    near = others("region", (1, -1, 2, -2))
    meet(same + near)
    sems = (send_sems, recv_sems)
    copies = [
        send(partial_ref, landed.at[k], sems, k, *peer) for k, peer in enumerate(same)
    ]
    value = partial_ref[...]
    for k, copy in enumerate(copies):
        copy.wait()
        value = value + landed[k]
    total[...] = value
    base = len(same)
    copies = [
        send(total.at[pl.ds(1, 2)], up, sems, base, *near[0]),
        send(total.at[pl.ds(0, 2)], down, sems, base + 1, *near[1]),
        send(total.at[pl.ds(2, 1)], far_up, sems, base + 2, *near[2]),
        send(total.at[pl.ds(0, 1)], far_down, sems, base + 3, *near[3]),
    ]
    for copy in copies:
        copy.wait()
    modelled = (
        total[0] + up[0] + far_up[0], total[1] + up[1] + down[0], total[2] + down[1] + far_down[0]
    )
    for q in range(3):
        out_ref[q] = lists_ref[q, 2] * (modelled[q] - lists_ref[q, 1])


def chunks_of(count):
    return lax.div(count + CHUNK - 1, CHUNK)


def span_of(index):
    return pl.ds(pl.multiple_of(index * CHUNK, CHUNK), CHUNK)


def collect_kernel(
    shape, counts_ref, starts_ref, rank_ref, values_ref, members_hbm, list_ref, mv_ref, found_ref,
    members_ref, fetch_sem
):
    fetch = pltpu.make_async_copy(members_hbm, members_ref, fetch_sem)
    fetch.start()
    _, _, _, width_y = shape
    group = math.prod(shape[:3])
    per_dev = members_ref.shape[0] // group
    count = counts_ref[0, 1]
    blocks, _, block = rank_ref.shape
    list_ref[...] = jnp.zeros_like(list_ref)
    mv_ref[...] = jnp.zeros_like(mv_ref)
    fetch.wait()

    @pl.loop(0, chunks_of(count))
    def _(index):
        base = index * CHUNK
        slot = base + lax.broadcasted_iota(jnp.int32, (CHUNK, block), 0)
        found_ref[...] = jnp.zeros_like(found_ref)

        @pl.loop(0, blocks)
        def _(source):
            @pl.when((starts_ref[0, source] < base + CHUNK) & (starts_ref[0, source + 1] > base))
            def _():
                pick = (rank_ref[source] == slot).astype(jnp.float32).astype(jnp.bfloat16)
                value = values_ref[source]
                first = value.astype(jnp.bfloat16).astype(jnp.float32)
                rest = value - first
                second = rest.astype(jnp.bfloat16).astype(jnp.float32)
                third = rest - second
                parts = jnp.concatenate([first, second, third], axis=0).astype(jnp.bfloat16)
                found_ref[...] += dot_nt(parts, pick)

        found = found_ref[0:8] + found_ref[8:16] + found_ref[16:24]
        for row in range(3):
            list_ref[row, :, span_of(index)] = found[row:row + 1]
        cell = found[0:1].astype(jnp.int32)
        y, column, _, _ = cells_of(cell, shape)
        live = base + lax.broadcasted_iota(jnp.int32, (1, CHUNK), 1) < count
        column = jnp.where(live, column, -1)
        hot = (lax.broadcasted_iota(jnp.int32, (width_y, CHUNK), 0) == y)
        hot = hot.astype(jnp.float32).astype(jnp.bfloat16)
        wanted = lax.broadcasted_iota(jnp.int32, (group, CHUNK), 0) == column
        rows = []
        for m in range(0, per_dev, 4):
            here = dot(members_ref[m * group:(m + 4) * group], hot)
            for k in range(4):
                one = jnp.where(wanted, here[k * group:(k + 1) * group], 0.0)
                rows.append(jnp.sum(one, axis=0, keepdims=True))
        mv_ref[:, span_of(index)] = jnp.concatenate(rows, axis=0).astype(jnp.bfloat16)


def footprint(shape, cell, side):
    _, lev, width_x, width_y = shape
    y, _, x, level = cells_of(cell, shape)
    hot = (lax.broadcasted_iota(jnp.int32, (width_y, CHUNK), 0) == y)
    hot = hot.astype(jnp.float32).astype(jnp.bfloat16)
    row = lax.broadcasted_iota(jnp.int32, (lev * width_x, CHUNK), 0)
    step = x + (side - 1) * width_x - lax.rem(row, width_x)
    dist = step.astype(jnp.float32)
    near = (jnp.abs(step) <= HALF) & (lax.div(row, width_x) == level)
    return hot, jnp.where(near, jnp.exp(-dist * dist / 72.0) * (1.0 / NORM), 0.0)


def sample_kernel(shape, counts_ref, list_ref, mv_ref, high_ref, low_ref, out_ref):
    plane = shape[1] * shape[2]
    per_dev = mv_ref.shape[1]
    group = max(1, 512 // plane)
    out_ref[...] = jnp.zeros_like(out_ref)
    for side in range(3):

        @pl.loop(0, chunks_of(counts_ref[0, side]))
        def _(index):
            span = span_of(index)
            hot, across = footprint(shape, list_ref[side, 0, :, span].astype(jnp.int32), side)
            mv = mv_ref[side, :, span].astype(jnp.float32)
            total = jnp.zeros((plane, CHUNK), jnp.float32)
            for m in range(0, per_dev, group):
                rows = slice(m * plane, (m + group) * plane)
                here = dot(high_ref[rows], hot) + dot(low_ref[rows], hot)
                for k in range(group):
                    total += here[k * plane:(k + 1) * plane] * mv[m + k:m + k + 1]
            out_ref[side, :, span] = jnp.sum(total * across, axis=0, keepdims=True)


def spread_kernel(
    shape, counts_ref, list_ref, mv_ref, weighted_ref, control_hbm, high_ref, low_ref, out_hbm,
    acc, control_ref, fetch_sem, store_sems
):
    fetch = pltpu.make_async_copy(control_hbm, control_ref, fetch_sem)
    fetch.start()
    plane = shape[1] * shape[2]
    per_dev = mv_ref.shape[1]
    group = max(1, 512 // plane)
    acc[...] = jnp.zeros_like(acc)
    for side in range(3):

        @pl.loop(0, chunks_of(counts_ref[0, side]))
        def _(index):
            span = span_of(index)
            hot, across = footprint(shape, list_ref[side, 0, :, span].astype(jnp.int32), side)
            scaled = mv_ref[side, :, span].astype(jnp.float32) * weighted_ref[side, :, span]
            for m in range(0, per_dev, group):
                rows = slice(m * plane, (m + group) * plane)
                terms = [across * scaled[m + k:m + k + 1] for k in range(group)]
                high, low = halves(jnp.concatenate(terms, axis=0))
                acc[rows] += dot_nt(high, hot) + dot_nt(low, hot)

    fetch.wait()
    stores = []
    for k in range(acc.shape[0] // 256):
        rows = pl.ds(k * 256, 256)
        acc[rows] = control_ref[rows] + filter_rows(acc[rows], high_ref[...], low_ref[...])
        stores.append(pltpu.make_async_copy(acc.at[rows], out_hbm.at[rows], store_sems.at[k]))
        stores[-1].start()
    for store in stores:
        store.wait()


def local(control, members, obs_tile, obs_cell, innovation, obs_weight):
    per_dev, times, lev, width_x, width_y = members.shape
    shape = (times, lev, width_x, width_y)
    rows = per_dev * lev * width_x
    regions = lax.axis_size("region")
    shares = lax.axis_size("member")
    obs_dev = obs_cell.shape[0]
    capacity = regions * (4 * obs_dev // regions)
    slots = -(-capacity // CHUNK) * CHUNK
    f32, bf16, i32 = jnp.float32, jnp.bfloat16, jnp.int32
    like = jax.ShapeDtypeStruct
    vmem = pl.BlockSpec(memory_space=pltpu.VMEM)
    hbm = pl.BlockSpec(memory_space=pl.ANY)
    smem = pl.BlockSpec(memory_space=pltpu.SMEM)
    plain = pltpu.CompilerParams(vmem_limit_bytes=LIMIT)
    sems = pltpu.SemaphoreType.DMA

    def remote(number):
        return pltpu.CompilerParams(
            vmem_limit_bytes=LIMIT, collective_id=number, has_side_effects=True
        )

    flat = control.reshape(rows, width_y)
    span = -(-(regions + 1) // 128) * 128
    field, table = like((rows, width_y), bf16), like((width_y, width_y), bf16)
    every, rank, starts, counts, field_high, field_low, table_high, table_low = pl.pallas_call(
        functools.partial(gather_kernel, regions),
        in_specs=[vmem] * 4 + [hbm],
        out_specs=[vmem] * 8,
        out_shape=[
            like((regions, 8, obs_dev), f32), like((regions, 1, obs_dev), i32),
            like((1, span), i32), like((1, 128), i32), field, field, table, table,
        ],
        scratch_shapes=[
            pltpu.VMEM((8, obs_dev), f32), pltpu.VMEM((rows, width_y), f32),
            pltpu.VMEM((regions - 1, 8, obs_dev), f32), sems((regions - 1,)), sems((regions - 1,)),
            sems(()),
        ],
        compiler_params=remote(0),
        name="gather_observations",
    )(*(v.reshape(1, obs_dev) for v in (obs_cell, innovation, obs_weight, obs_tile)), flat)

    listed, mv = pl.pallas_call(
        functools.partial(collect_kernel, shape),
        in_specs=[smem] * 2 + [vmem] * 2 + [hbm],
        out_specs=[vmem] * 2,
        out_shape=[like((3, 1, slots), f32), like((per_dev, slots), bf16)],
        scratch_shapes=[
            pltpu.VMEM((24, CHUNK), f32),
            pltpu.VMEM((per_dev * times * lev * width_x, width_y), bf16),
            sems(()),
        ],
        compiler_params=plain,
        name="collect_members",
    )(counts, starts, rank, every, members.reshape(-1, width_y))

    lists, mvs = pl.pallas_call(
        exchange_kernel,
        in_specs=[vmem] * 2,
        out_specs=[vmem] * 2,
        out_shape=[like((3, 3, 1, slots), f32), like((3, per_dev, slots), bf16)],
        scratch_shapes=[
            pltpu.VMEM((2, 3, 1, slots), f32), pltpu.VMEM((2, per_dev, slots), bf16),
            sems((4,)), sems((4,)),
        ],
        compiler_params=remote(1),
        name="exchange_members",
    )(listed, mv)

    partial = pl.pallas_call(
        functools.partial(sample_kernel, shape),
        in_specs=[smem] + [vmem] * 4,
        out_specs=vmem,
        out_shape=like((3, 1, slots), f32),
        compiler_params=plain,
        name="sample_increment",
    )(counts, lists, mvs, field_high, field_low)

    weighted = pl.pallas_call(
        functools.partial(combine_kernel, shares),
        in_specs=[vmem] * 2,
        out_specs=vmem,
        out_shape=like((3, 1, slots), f32),
        scratch_shapes=[
            pltpu.VMEM((shares - 1, 3, 1, slots), f32), pltpu.VMEM((3, 1, slots), f32),
            pltpu.VMEM((2, 1, slots), f32), pltpu.VMEM((2, 1, slots), f32),
            pltpu.VMEM((1, 1, slots), f32), pltpu.VMEM((1, 1, slots), f32),
            sems((shares + 3,)), sems((shares + 3,)),
        ],
        compiler_params=remote(2),
        name="combine_samples",
    )(partial, lists)

    result = pl.pallas_call(
        functools.partial(spread_kernel, shape),
        in_specs=[smem] + [vmem] * 3 + [hbm] + [vmem] * 2,
        out_specs=hbm,
        out_shape=like((rows, width_y), f32),
        scratch_shapes=[
            pltpu.VMEM((rows, width_y), f32), pltpu.VMEM((rows, width_y), f32),
            sems(()), sems((rows // 256,)),
        ],
        compiler_params=plain,
        name="spread_adjoint",
    )(counts, lists, mvs, weighted, flat, table_high, table_low)
    return result.reshape(control.shape)


def solution(mesh):
    placed = (
        P("member", None, "region", None),
        P("member", None, None, "region", None),
        P("region", None),
        P("region"),
        P("region"),
        P("region"),
    )
    return jax.shard_map(
        local,
        mesh=mesh,
        in_specs=placed,
        out_specs=P("member", None, "region", None),
        check_vma=False,
    )
```

```python
import functools
import math

import jax
import jax.numpy as jnp
from jax import lax
from jax.experimental import pallas as pl
from jax.experimental.pallas import tpu as pltpu
from jax.sharding import PartitionSpec as P

HALF = 15
CHUNK = 256
NORM = math.sqrt(sum(math.exp(-e * e / 36.0) for e in range(-HALF, HALF + 1)))
LIMIT = 63 * 1024 * 1024
MESH = pl.DeviceIdType.MESH
NT_DIMS = (((1,), (1,)), ((), ()))


def band_table(count):
    shape = (count, count)
    step = lax.broadcasted_iota(jnp.int32, shape, 1) - lax.broadcasted_iota(jnp.int32, shape, 0)
    dist = step.astype(jnp.float32)
    return jnp.where(jnp.abs(step) <= HALF, jnp.exp(-dist * dist / 72.0) * (1.0 / NORM), 0.0)


def dot(a, b):
    return jnp.dot(a, b, preferred_element_type=jnp.float32)


def dot_nt(a, b):
    return lax.dot_general(a, b, NT_DIMS, preferred_element_type=jnp.float32)


def halves(value):
    high = value.astype(jnp.bfloat16)
    low = (value - high.astype(jnp.float32)).astype(jnp.bfloat16)
    return high, low


def filter_rows(value, table_high, table_low):
    high, low = halves(value)
    return dot(high, table_high) + (dot(high, table_low) + dot(low, table_high))


def cells_of(cell, shape):
    _, lev, width_x, width_y = shape
    y = lax.rem(cell, width_y)
    column = lax.div(cell, width_y)
    x = lax.rem(column, width_x)
    level = lax.rem(lax.div(column, width_x), lev)
    return y, column, x, level


def meet(peers):
    barrier = pltpu.get_barrier_semaphore()
    for axis, peer in peers:
        pl.semaphore_signal(barrier, inc=1, device_id={axis: peer}, device_id_type=MESH)
    pl.semaphore_wait(barrier, len(peers))


def send(source, target, sems, index, axis, peer):
    copy = pltpu.make_async_remote_copy(
        src_ref=source,
        dst_ref=target,
        send_sem=sems[0].at[index],
        recv_sem=sems[1].at[index],
        device_id={axis: peer},
        device_id_type=MESH,
    )
    copy.start()
    return copy


def others(axis, offsets):
    me, count = lax.axis_index(axis), lax.axis_size(axis)
    return [(axis, lax.rem(me + count + by, count)) for by in offsets]


def gather_kernel(
    regions, cell_ref, innovation_ref, weight_ref, tile_ref, control_hbm, every_ref, rank_ref, starts_ref, counts_ref,
    out_high_ref, out_low_ref, high_ref, low_ref, packed_ref, control_ref, landed,
    send_sems, recv_sems, fetch_sem
):
    fetch = pltpu.make_async_copy(control_hbm, control_ref, fetch_sem)
    fetch.start()
    packed_ref[...] = jnp.zeros_like(packed_ref)
    packed_ref[0:1] = cell_ref[...].astype(jnp.float32)
    packed_ref[1:2] = innovation_ref[...]
    packed_ref[2:3] = weight_ref[...]
    packed_ref[3:4] = tile_ref[...].astype(jnp.float32)
    peers = others("region", range(1, regions))
    meet(peers)
    sems = (send_sems, recv_sems)
    copies = [
        send(packed_ref, landed.at[k], sems, k, *peer) for k, peer in enumerate(peers)
    ]
    high_ref[...], low_ref[...] = halves(band_table(control_ref.shape[1]))
    fetch.wait()
    for r in range(0, control_ref.shape[0], 256):
        rows = slice(r, r + 256)
        filtered = filter_rows(control_ref[rows], high_ref[...], low_ref[...])
        out_high_ref[rows], out_low_ref[rows] = halves(filtered)
    width = packed_ref.shape[1]
    every_ref[0] = packed_ref[...]
    for k, copy in enumerate(copies):
        copy.wait()
        every_ref[k + 1] = landed[k]

    me = lax.axis_index("region")
    owner = [every_ref[k, 3:4] for k in range(regions)]
    mine = [(o.astype(jnp.int32) == me).astype(jnp.float32) for o in owner]
    mask = jnp.concatenate(mine, axis=0)
    order = lax.broadcasted_iota(jnp.int32, (width, width), 0)
    upper = order <= lax.broadcasted_iota(jnp.int32, (width, width), 1)
    inside = dot(mask.astype(jnp.bfloat16), upper.astype(jnp.float32).astype(jnp.bfloat16))
    lane = lax.broadcasted_iota(jnp.int32, starts_ref.shape, 1)
    starts = jnp.zeros(starts_ref.shape, jnp.float32)
    before = jnp.zeros((1, 1), jnp.float32)
    for k in range(regions):
        starts = jnp.where(lane == k, before, starts)
        rank = jnp.where(mine[k] > 0.5, inside[k:k + 1] + before - 1.0, -1.0)
        rank_ref[k] = rank.astype(jnp.int32)
        before = before + jnp.sum(mine[k], axis=1, keepdims=True)
    starts_ref[...] = jnp.where(lane == regions, before, starts).astype(jnp.int32)
    lane = lax.broadcasted_iota(jnp.int32, counts_ref.shape, 1)
    counts = jnp.zeros(counts_ref.shape, jnp.float32)
    tiles = jnp.concatenate(owner, axis=0).astype(jnp.int32)
    for side in range(3):
        tile = lax.rem(me + regions + side - 1, regions)
        named = jnp.sum((tiles == tile).astype(jnp.float32), axis=0, keepdims=True)
        counts = jnp.where(lane == side, jnp.sum(named, axis=1, keepdims=True), counts)
    counts_ref[...] = counts.astype(jnp.int32)


def exchange_kernel(list_ref, mv_ref, lists_ref, mvs_ref, land_list, land_mv, send_sems, recv_sems):
    peers = others("region", (1, -1))
    meet(peers)
    sems = (send_sems, recv_sems)
    copies = []
    for k, peer in enumerate(peers):
        copies.append(send(mv_ref, land_mv.at[k], sems, 2 * k, *peer))
        copies.append(send(list_ref, land_list.at[k], sems, 2 * k + 1, *peer))
    lists_ref[1] = list_ref[...]
    mvs_ref[1] = mv_ref[...]
    for copy in copies:
        copy.wait()
    for k in range(2):
        lists_ref[2 * k] = land_list[k]
        mvs_ref[2 * k] = land_mv[k]


def combine_kernel(
    members, partial_ref, lists_ref, out_ref, landed, total, up, down, far_up, far_down,
    send_sems, recv_sems
):
    same = others("member", range(1, members))
    near = others("region", (1, -1, 2, -2))
    meet(same + near)
    sems = (send_sems, recv_sems)
    copies = [
        send(partial_ref, landed.at[k], sems, k, *peer) for k, peer in enumerate(same)
    ]
    value = partial_ref[...]
    for k, copy in enumerate(copies):
        copy.wait()
        value = value + landed[k]
    total[...] = value
    base = len(same)
    copies = [
        send(total.at[pl.ds(1, 2)], up, sems, base, *near[0]),
        send(total.at[pl.ds(0, 2)], down, sems, base + 1, *near[1]),
        send(total.at[pl.ds(2, 1)], far_up, sems, base + 2, *near[2]),
        send(total.at[pl.ds(0, 1)], far_down, sems, base + 3, *near[3]),
    ]
    for copy in copies:
        copy.wait()
    modelled = (
        total[0] + up[0] + far_up[0], total[1] + up[1] + down[0], total[2] + down[1] + far_down[0]
    )
    for q in range(3):
        out_ref[q] = lists_ref[q, 2] * (modelled[q] - lists_ref[q, 1])


def chunks_of(count):
    return lax.div(count + CHUNK - 1, CHUNK)


def span_of(index):
    return pl.ds(pl.multiple_of(index * CHUNK, CHUNK), CHUNK)


def collect_kernel(
    shape, counts_ref, starts_ref, rank_ref, values_ref, members_hbm, list_ref, mv_ref, found_ref,
    members_ref, fetch_sem
):
    fetch = pltpu.make_async_copy(members_hbm, members_ref, fetch_sem)
    fetch.start()
    _, _, _, width_y = shape
    group = math.prod(shape[:3])
    per_dev = members_ref.shape[0] // group
    count = counts_ref[0, 1]
    blocks, _, block = rank_ref.shape
    list_ref[...] = jnp.zeros_like(list_ref)
    mv_ref[...] = jnp.zeros_like(mv_ref)
    fetch.wait()

    @pl.loop(0, chunks_of(count))
    def _(index):
        base = index * CHUNK
        slot = base + lax.broadcasted_iota(jnp.int32, (CHUNK, block), 0)
        found_ref[...] = jnp.zeros_like(found_ref)

        @pl.loop(0, blocks)
        def _(source):
            @pl.when((starts_ref[0, source] < base + CHUNK) & (starts_ref[0, source + 1] > base))
            def _():
                pick = (rank_ref[source] == slot).astype(jnp.float32).astype(jnp.bfloat16)
                value = values_ref[source]
                first = value.astype(jnp.bfloat16).astype(jnp.float32)
                rest = value - first
                second = rest.astype(jnp.bfloat16).astype(jnp.float32)
                third = rest - second
                parts = jnp.concatenate([first, second, third], axis=0).astype(jnp.bfloat16)
                found_ref[...] += dot_nt(parts, pick)

        found = found_ref[0:8] + found_ref[8:16] + found_ref[16:24]
        for row in range(3):
            list_ref[row, :, span_of(index)] = found[row:row + 1]
        cell = found[0:1].astype(jnp.int32)
        y, column, _, _ = cells_of(cell, shape)
        live = base + lax.broadcasted_iota(jnp.int32, (1, CHUNK), 1) < count
        column = jnp.where(live, column, -1)
        hot = (lax.broadcasted_iota(jnp.int32, (width_y, CHUNK), 0) == y)
        hot = hot.astype(jnp.float32).astype(jnp.bfloat16)
        wanted = lax.broadcasted_iota(jnp.int32, (group, CHUNK), 0) == column
        rows = []
        for m in range(0, per_dev, 4):
            here = dot(members_ref[m * group:(m + 4) * group], hot)
            for k in range(4):
                one = jnp.where(wanted, here[k * group:(k + 1) * group], 0.0)
                rows.append(jnp.sum(one, axis=0, keepdims=True))
        mv_ref[:, span_of(index)] = jnp.concatenate(rows, axis=0).astype(jnp.bfloat16)


def footprint(shape, cell, side):
    _, lev, width_x, width_y = shape
    y, _, x, level = cells_of(cell, shape)
    hot = (lax.broadcasted_iota(jnp.int32, (width_y, CHUNK), 0) == y)
    hot = hot.astype(jnp.float32).astype(jnp.bfloat16)
    row = lax.broadcasted_iota(jnp.int32, (lev * width_x, CHUNK), 0)
    step = x + (side - 1) * width_x - lax.rem(row, width_x)
    dist = step.astype(jnp.float32)
    near = (jnp.abs(step) <= HALF) & (lax.div(row, width_x) == level)
    return hot, jnp.where(near, jnp.exp(-dist * dist / 72.0) * (1.0 / NORM), 0.0)


def sample_kernel(shape, counts_ref, list_ref, mv_ref, high_ref, low_ref, out_ref):
    plane = shape[1] * shape[2]
    per_dev = mv_ref.shape[1]
    group = max(1, 512 // plane)
    out_ref[...] = jnp.zeros_like(out_ref)
    for side in range(3):

        @pl.loop(0, chunks_of(counts_ref[0, side]))
        def _(index):
            span = span_of(index)
            hot, across = footprint(shape, list_ref[side, 0, :, span].astype(jnp.int32), side)
            mv = mv_ref[side, :, span].astype(jnp.float32)
            total = jnp.zeros((plane, CHUNK), jnp.float32)
            for m in range(0, per_dev, group):
                rows = slice(m * plane, (m + group) * plane)
                here = dot(high_ref[rows], hot) + dot(low_ref[rows], hot)
                for k in range(group):
                    total += here[k * plane:(k + 1) * plane] * mv[m + k:m + k + 1]
            out_ref[side, :, span] = jnp.sum(total * across, axis=0, keepdims=True)


def spread_kernel(
    shape, counts_ref, list_ref, mv_ref, weighted_ref, control_hbm, high_ref, low_ref, out_hbm,
    acc, control_ref, fetch_sem, store_sems
):
    fetch = pltpu.make_async_copy(control_hbm, control_ref, fetch_sem)
    fetch.start()
    plane = shape[1] * shape[2]
    per_dev = mv_ref.shape[1]
    group = max(1, 512 // plane)
    acc[...] = jnp.zeros_like(acc)
    for side in range(3):

        @pl.loop(0, chunks_of(counts_ref[0, side]))
        def _(index):
            span = span_of(index)
            hot, across = footprint(shape, list_ref[side, 0, :, span].astype(jnp.int32), side)
            scaled = mv_ref[side, :, span].astype(jnp.float32) * weighted_ref[side, :, span]
            for m in range(0, per_dev, group):
                rows = slice(m * plane, (m + group) * plane)
                terms = [across * scaled[m + k:m + k + 1] for k in range(group)]
                high, low = halves(jnp.concatenate(terms, axis=0))
                acc[rows] += dot_nt(high, hot) + dot_nt(low, hot)

    fetch.wait()
    stores = []
    for k in range(acc.shape[0] // 256):
        rows = pl.ds(k * 256, 256)
        acc[rows] = control_ref[rows] + filter_rows(acc[rows], high_ref[...], low_ref[...])
        stores.append(pltpu.make_async_copy(acc.at[rows], out_hbm.at[rows], store_sems.at[k]))
        stores[-1].start()
    for store in stores:
        store.wait()


def local(control, members, obs_tile, obs_cell, innovation, obs_weight):
    per_dev, times, lev, width_x, width_y = members.shape
    shape = (times, lev, width_x, width_y)
    rows = per_dev * lev * width_x
    regions = lax.axis_size("region")
    shares = lax.axis_size("member")
    obs_dev = obs_cell.shape[0]
    capacity = regions * (4 * obs_dev // regions)
    slots = -(-capacity // CHUNK) * CHUNK
    f32, bf16, i32 = jnp.float32, jnp.bfloat16, jnp.int32
    like = jax.ShapeDtypeStruct
    vmem = pl.BlockSpec(memory_space=pltpu.VMEM)
    hbm = pl.BlockSpec(memory_space=pl.ANY)
    smem = pl.BlockSpec(memory_space=pltpu.SMEM)
    plain = pltpu.CompilerParams(vmem_limit_bytes=LIMIT)
    sems = pltpu.SemaphoreType.DMA

    def remote(number):
        return pltpu.CompilerParams(
            vmem_limit_bytes=LIMIT, collective_id=number, has_side_effects=True
        )

    flat = control.reshape(rows, width_y)
    span = -(-(regions + 1) // 128) * 128
    field, table = like((rows, width_y), bf16), like((width_y, width_y), bf16)
    every, rank, starts, counts, field_high, field_low, table_high, table_low = pl.pallas_call(
        functools.partial(gather_kernel, regions),
        in_specs=[vmem] * 4 + [hbm],
        out_specs=[vmem] * 8,
        out_shape=[
            like((regions, 8, obs_dev), f32), like((regions, 1, obs_dev), i32),
            like((1, span), i32), like((1, 128), i32), field, field, table, table,
        ],
        scratch_shapes=[
            pltpu.VMEM((8, obs_dev), f32), pltpu.VMEM((rows, width_y), f32),
            pltpu.VMEM((regions - 1, 8, obs_dev), f32), sems((regions - 1,)), sems((regions - 1,)),
            sems(()),
        ],
        compiler_params=remote(0),
        name="gather_observations",
    )(*(v.reshape(1, obs_dev) for v in (obs_cell, innovation, obs_weight, obs_tile)), flat)

    listed, mv = pl.pallas_call(
        functools.partial(collect_kernel, shape),
        in_specs=[smem] * 2 + [vmem] * 2 + [hbm],
        out_specs=[vmem] * 2,
        out_shape=[like((3, 1, slots), f32), like((per_dev, slots), bf16)],
        scratch_shapes=[
            pltpu.VMEM((24, CHUNK), f32),
            pltpu.VMEM((per_dev * times * lev * width_x, width_y), bf16),
            sems(()),
        ],
        compiler_params=plain,
        name="collect_members",
    )(counts, starts, rank, every, members.reshape(-1, width_y))

    lists, mvs = pl.pallas_call(
        exchange_kernel,
        in_specs=[vmem] * 2,
        out_specs=[vmem] * 2,
        out_shape=[like((3, 3, 1, slots), f32), like((3, per_dev, slots), bf16)],
        scratch_shapes=[
            pltpu.VMEM((2, 3, 1, slots), f32), pltpu.VMEM((2, per_dev, slots), bf16),
            sems((4,)), sems((4,)),
        ],
        compiler_params=remote(1),
        name="exchange_members",
    )(listed, mv)

    partial = pl.pallas_call(
        functools.partial(sample_kernel, shape),
        in_specs=[smem] + [vmem] * 4,
        out_specs=vmem,
        out_shape=like((3, 1, slots), f32),
        compiler_params=plain,
        name="sample_increment",
    )(counts, lists, mvs, field_high, field_low)

    weighted = pl.pallas_call(
        functools.partial(combine_kernel, shares),
        in_specs=[vmem] * 2,
        out_specs=vmem,
        out_shape=like((3, 1, slots), f32),
        scratch_shapes=[
            pltpu.VMEM((shares - 1, 3, 1, slots), f32), pltpu.VMEM((3, 1, slots), f32),
            pltpu.VMEM((2, 1, slots), f32), pltpu.VMEM((2, 1, slots), f32),
            pltpu.VMEM((1, 1, slots), f32), pltpu.VMEM((1, 1, slots), f32),
            sems((shares + 3,)), sems((shares + 3,)),
        ],
        compiler_params=remote(2),
        name="combine_samples",
    )(partial, lists)

    result = pl.pallas_call(
        functools.partial(spread_kernel, shape),
        in_specs=[smem] + [vmem] * 3 + [hbm] + [vmem] * 2,
        out_specs=hbm,
        out_shape=like((rows, width_y), f32),
        scratch_shapes=[
            pltpu.VMEM((rows, width_y), f32), pltpu.VMEM((rows, width_y), f32),
            sems(()), sems((rows // 256,)),
        ],
        compiler_params=plain,
        name="spread_adjoint",
    )(counts, lists, mvs, weighted, flat, table_high, table_low)
    return result.reshape(control.shape)


def solution(mesh):
    placed = (
        P("member", None, "region", None),
        P("member", None, None, "region", None),
        P("region", None),
        P("region"),
        P("region"),
        P("region"),
    )
    return jax.shard_map(
        local,
        mesh=mesh,
        in_specs=placed,
        out_specs=P("member", None, "region", None),
        check_vma=False,
    )
```
